32 devices in a mesh: vol: 8 (over z, y), rep: 4 (over x, core).
Axes of the slice: x: 2, y: 2, z: 4, core: 2. Of those that a mesh axis runs over, the one named last changes fastest.
Arguments:
- features: bfloat16 [8, 32, 4, 8192], P('vol', None, None, 'rep'), may hold values from -6 to 6
- deltas: float32 [8, 4, 8192], P('vol', None, 'rep'), may hold values from 0.0125 to 0.125
- counts: int32 [8, 8192], P('vol', 'rep'), may hold values from 0 to 4
- order_rank: int32 [8192, 8], P('rep'), may hold values from 0 to 7, each once within a row
- cotangent: float32 [3, 8192], P(None, 'rep'), may hold values from -6 to 6
- first_weight: bfloat16 [8, 32, 256], P('vol'), may hold values from -1.5 to 1.5
- middle_weight: bfloat16 [8, 2, 256, 256], P('vol'), may hold values from -0.5 to 0.5
- last_weight: bfloat16 [8, 256, 4], P('vol'), may hold values from -0.375 to 0.375
Outputs:
- first_grad: float32 [8, 32, 256], P('vol')
- middle_grad: float32 [8, 2, 256, 256], P('vol')
- last_grad: float32 [8, 256, 4], P('vol')
The draws below stay inside these ranges and needn't reach their ends.
Inputs may be any that keep to these rules, and one draw needn't show every extreme that they name: `order_rank`: each ray's row holds every number of 0 .. 7 once.
All inputs are finite; a program needn't handle non-finite values.
Results may differ from the reference program's by a relative error of at most 0.0083.
Values sent between devices are 32-bit elements; how exact they have to be, the bound alone decides.
A program may use at most 128 MiB of HBM per device.

```python
import math
import jax
import jax.numpy as jnp
from jax import lax

FEAT = 32
W = 256
HID = 2
SAMP = 4
NV = 8
NR = 8192


def touch_ends(array, stream_key, least, largest):
    longest = array.shape.index(max(array.shape))
    spots = []
    for shift in (0, 1):
        where = [jax.random.randint(jax.random.fold_in(stream_key, axis), (), 0, length) for axis, length in enumerate(array.shape)]
        where[longest] = (where[longest] + shift) % array.shape[longest]
        spots.append(tuple(where))
    return array.at[spots[0]].set(least).at[spots[1]].set(largest)


def levels(own_key, dims, pieces, low, top_value):
    level = 1.0
    for axis_at, shards_of in pieces:
        steps = jax.random.uniform(jax.random.fold_in(jax.random.fold_in(own_key, 6), axis_at), (shards_of,), jnp.float32, low / len(pieces), top_value / len(pieces))
        level = level * jnp.repeat(jnp.exp(steps), dims[axis_at] // shards_of).reshape((-1,) + (1,) * (len(dims) - 1 - axis_at))
    return level


def gaussian(key, extent, width, reach, shards=(), kind=jnp.bfloat16):
    gain = levels(key, extent, shards, -0.22, 0.18) if shards else 1.0
    result = jax.random.normal(key, extent, jnp.float32) * width * gain
    return jnp.minimum(jnp.maximum(result, -reach), reach).astype(kind)


def setup_inputs(seed: int = 0) -> dict:
    streams_of = jax.random.split(jax.random.key(seed), 9)
    return {
        "features": gaussian(streams_of[0], (NV, FEAT, SAMP, NR), 1.0, 6.0, ((0, 8), (3, 4))),
        "deltas": jnp.clip(jnp.exp(math.log(0.125) - 2.3025851 * jax.random.uniform(streams_of[1], (NV, SAMP, NR), jnp.float32) ** levels(streams_of[1], (NV, SAMP, NR), ((0, 8), (2, 4)), -0.2, 0.2)), 0.0125, 0.125),
        "counts": touch_ends(jax.random.randint(streams_of[2], (NV, NR), 0, SAMP + 1), jax.random.fold_in(streams_of[2], 1), 0, SAMP).astype(jnp.int32),
        "order_rank": jax.vmap(lambda own: jax.random.permutation(own, NV))(jax.random.split(streams_of[3], NR)).reshape((NR, NV)).astype(jnp.int32),
        "cotangent": gaussian(streams_of[4], (3, NR), 1.0, 6.0, ((1, 4),), jnp.float32),
        "first_weight": gaussian(streams_of[5], (NV, FEAT, W), (FEAT // 2) ** -0.5, 1.5, ((0, 8),)),
        "middle_weight": gaussian(streams_of[6], (NV, HID, W, W), (W // 2) ** -0.5, 0.5, ((0, 8),)),
        "last_weight": gaussian(streams_of[7], (NV, W, 4), W ** -0.5, 0.375, ((0, 8),)),
    }


def contract_first(matrix, rows):
    return lax.dot_general(matrix, rows, (((0,), (0,)), ((), ())), preferred_element_type=jnp.float32)

def contract_last(left, right):
    return lax.dot_general(left, right, (((1,), (1,)), ((), ())), preferred_element_type=jnp.float32)

def silu_grad(pre):
    logistic = jax.nn.sigmoid(pre)
    return logistic * (1.0 + pre * (1.0 - logistic))

def forward_network(samples, first_weight, middle_weight, last_weight):
    pre = contract_first(first_weight, samples)
    preacts = [pre]
    layer_inputs = [samples]
    hidden = jax.nn.silu(pre).astype(jnp.bfloat16)
    for depth in range(middle_weight.shape[0]):
        layer_inputs.append(hidden)
        pre = contract_first(middle_weight[depth], hidden)
        preacts.append(pre)
        hidden = jax.nn.silu(pre).astype(jnp.bfloat16)
    layer_inputs.append(hidden)
    head_out = contract_first(last_weight, hidden)
    return (preacts, layer_inputs, head_out)

def render_segment(head_out, deltas, counts):
    density = jax.nn.softplus(head_out[0])
    albedo = jax.nn.sigmoid(head_out[1:])
    live = (lax.broadcasted_iota(jnp.int32, deltas.shape, 0) < counts[None, :]).astype(jnp.float32)
    optical = density * deltas * live
    reached = jnp.cumsum(optical, axis=0)
    passed = reached - optical
    leaving = jnp.exp(-reached)
    sample_weight = jnp.exp(-passed) - leaving
    colour = lax.optimization_barrier(jnp.sum(sample_weight[None] * albedo, axis=1))
    logt = -reached[-1]
    return (colour, logt, (albedo, leaving, sample_weight, live))

def head_gradient(head_out, deltas, saved, grad_colour, grad_logt):
    albedo, leaving, sample_weight, live = saved
    facing = lax.optimization_barrier(jnp.sum(grad_colour[:, None, :] * albedo, axis=0))
    weighted = facing * sample_weight
    later = lax.optimization_barrier(jnp.sum(weighted, axis=0))[None] - jnp.cumsum(weighted, axis=0)
    doptical = facing * leaving - later - grad_logt[None]
    d_density = doptical * deltas * live * jax.nn.sigmoid(head_out[0])
    d_albedo = sample_weight[None] * grad_colour[:, None, :] * albedo * (1.0 - albedo)
    return jnp.concatenate([d_density[None], d_albedo], axis=0).astype(jnp.bfloat16)

def network_gradients(preacts, layer_inputs, head_grad, middle_weight, last_weight, reducers):
    last_grad = reducers[0](contract_last(layer_inputs[-1], head_grad))
    back = (jnp.dot(last_weight, head_grad, preferred_element_type=jnp.float32) * silu_grad(preacts[-1])).astype(jnp.bfloat16)
    hidden_grads = []
    for depth in reversed(range(middle_weight.shape[0])):
        hidden_grads.append(reducers[1](contract_last(layer_inputs[depth + 1], back)))
        back = (jnp.dot(middle_weight[depth], back, preferred_element_type=jnp.float32) * silu_grad(preacts[depth])).astype(jnp.bfloat16)
    first_grad = reducers[2](contract_last(layer_inputs[0], back))
    middle_grad = jnp.stack(hidden_grads[::-1], axis=0)
    return (first_grad, middle_grad, last_grad)

def composite_rays(segments, rank_rows, cotangent):
    logs = segments[:, 3]

    def add_log(index, total):
        other = lax.dynamic_index_in_dim(rank_rows, index, 0, keepdims=True)
        term = lax.dynamic_index_in_dim(logs, index, 0, keepdims=True)
        return total + jnp.where(other < rank_rows, term, 0.0)
    summed = lax.fori_loop(0, rank_rows.shape[0], add_log, jnp.zeros(rank_rows.shape, jnp.float32))
    prefix = jnp.exp(summed)
    facing = lax.optimization_barrier(jnp.sum(cotangent[None] * segments[:, :3], axis=1)) * prefix

    def add_behind(index, total):
        other = lax.dynamic_index_in_dim(rank_rows, index, 0, keepdims=True)
        term = lax.dynamic_index_in_dim(facing, index, 0, keepdims=True)
        return total + jnp.where(other > rank_rows, term, 0.0)
    behind = lax.fori_loop(0, rank_rows.shape[0], add_behind, jnp.zeros(rank_rows.shape, jnp.float32))
    return (prefix, behind)

def unchanged(value):
    return value

def reference(features, deltas, counts, order_rank, cotangent, first_weight, middle_weight, last_weight):

    def forward_one(bundle):
        feat_block, delta_block, count_block, weight_one, weight_two, weight_three = bundle
        samples = feat_block.reshape(feat_block.shape[0], -1)
        preacts, layer_inputs, head_out = forward_network(samples, weight_one, weight_two, weight_three)
        shaped = head_out.reshape(4, delta_block.shape[0], delta_block.shape[1])
        colour, logt, saved = render_segment(shaped, delta_block, count_block)
        return jnp.concatenate([colour, logt[None]], axis=0)
    segments = lax.map(forward_one, (features, deltas, counts, first_weight, middle_weight, last_weight))
    prefix, behind = composite_rays(segments, order_rank.T, cotangent)

    def backward_one(bundle):
        feat_block, delta_block, count_block, weight_one, weight_two, weight_three, own_prefix, own_behind = bundle
        samples = feat_block.reshape(feat_block.shape[0], -1)
        preacts, layer_inputs, head_out = forward_network(samples, weight_one, weight_two, weight_three)
        shaped = head_out.reshape(4, delta_block.shape[0], delta_block.shape[1])
        colour, logt, saved = render_segment(shaped, delta_block, count_block)
        grad_colour = own_prefix[None] * cotangent
        head_grad = head_gradient(shaped, delta_block, saved, grad_colour, own_behind).reshape(4, -1)
        return network_gradients(preacts, layer_inputs, head_grad, weight_two, weight_three, (unchanged, unchanged, unchanged))
    first_grad, middle_grad, last_grad = lax.map(backward_one, (features, deltas, counts, first_weight, middle_weight, last_weight, prefix, behind))
    return (first_grad, middle_grad, last_grad)
```

```python
import functools

import jax
import jax.numpy as jnp
from jax import lax
from jax.experimental import pallas as pl
from jax.experimental.pallas import tpu as pltpu
from jax.sharding import PartitionSpec as P

F32 = jnp.float32
BF16 = jnp.bfloat16
MESH = pl.DeviceIdType.MESH
HEADS = 16


def mul(left, right):
    return jnp.dot(left, right, preferred_element_type=F32)


def mul_nt(left, right):
    return lax.dot_general(left, right, (((1,), (1,)), ((), ())), preferred_element_type=F32)


def logistic(pre):
    return 0.5 * jnp.tanh(0.5 * pre) + 0.5


def activate(pre):
    gate = logistic(pre)
    hidden = pre * gate
    slope = gate + hidden * (1.0 - gate)
    return hidden.astype(BF16), slope.astype(BF16)


def kernel(
    dims,
    x_ref, deltas_ref, counts_ref, rank_ref, cot_ref,
    first_t_ref, mid_t_ref, last_t_ref, mid_ref, last_ref,
    out_ref,
    hidden, slope, gates, leaving, weights, spans, facing, seg, acc, half_in, half_x,
    seg_send, seg_recv, one_send, one_recv, two_send, two_recv, three_send, three_recv,
):
    volumes, replicas, samples, rays, depth, width, feats = dims
    chunk = rays // 4
    chunks = rays // chunk
    columns = samples * rays
    block = columns // 8
    pairs = replicas // 2
    mine = lax.axis_index("vol")
    rep = lax.axis_index("rep")
    core = lax.rem(rep, 2)
    across = rep // 2
    sibling = rep + 1 - 2 * core

    barrier = pltpu.get_barrier_semaphore()
    for k in range(1, volumes):
        pl.semaphore_signal(
            barrier, inc=1, device_id={"vol": lax.rem(mine + k, volumes)}, device_id_type=MESH
        )
    pl.semaphore_signal(barrier, inc=1, device_id={"rep": sibling}, device_id_type=MESH)
    for k in range(1, pairs):
        pl.semaphore_signal(
            barrier,
            inc=1,
            device_id={"rep": lax.rem(across + k, pairs) * 2 + core},
            device_id_type=MESH,
        )
    pl.semaphore_wait(barrier, volumes - 1 + pairs)

    def cols(start):
        return pl.ds(pl.multiple_of(start, 128), chunk)

    def seg_copy(q, k):
        part = cols(q * chunk)
        return pltpu.make_async_remote_copy(
            src_ref=seg.at[mine, :, part],
            dst_ref=seg.at[mine, :, part],
            send_sem=seg_send.at[q, k],
            recv_sem=seg_recv.at[q, k],
            device_id={"vol": lax.rem(mine + k, volumes)},
            device_id_type=MESH,
        )

    acc[...] = jnp.zeros_like(acc)

    def forward(q, carry):
        part = cols(q * chunk)
        cot = cot_ref[:, part]
        count = counts_ref[:, part]
        heads = []
        for s in range(samples):
            place = cols(s * rays + q * chunk)
            h, d = activate(mul(first_t_ref[...], x_ref[:, place]))
            hidden[0, :, place] = h
            slope[0, :, place] = d
            for k in range(depth):
                h, d = activate(mul(mid_t_ref[k], h))
                hidden[k + 1, :, place] = h
                slope[k + 1, :, place] = d
            heads.append(mul(last_t_ref[...], h)[:8])
        reached = jnp.zeros((1, chunk), F32)
        before = jnp.ones((1, chunk), F32)
        colour = jnp.zeros((1, chunk), F32)
        for s in range(samples):
            gate = logistic(heads[s])
            top = heads[s][0:1]
            density = jnp.maximum(top, 0.0) + jnp.log1p(jnp.exp(-jnp.abs(top)))
            span = jnp.where(s < count, deltas_ref[s : s + 1, part], 0.0)
            reached = reached + density * span
            after = jnp.exp(-reached)
            weight = before - after
            before = after
            face = jnp.sum(cot * gate, axis=0, keepdims=True)
            colour = colour + weight * face
            gates[s, :, part] = gate
            leaving[s : s + 1, part] = after
            weights[s : s + 1, part] = weight
            spans[s : s + 1, part] = span
            facing[s : s + 1, part] = face
        seg[mine, :, part] = jnp.concatenate([colour, -reached], axis=0)
        for k in range(1, volumes):
            seg_copy(q, k).start()
        return carry

    lax.fori_loop(0, chunks, forward, 0)

    def one(g, first, half):
        give = pl.multiple_of(first + (1 - core) * half, 8)
        return pltpu.make_async_remote_copy(
            src_ref=acc.at[pl.ds(give, half)],
            dst_ref=half_in.at[pl.ds(first // 2, half)],
            send_sem=one_send.at[g],
            recv_sem=one_recv.at[g],
            device_id={"rep": sibling},
            device_id_type=MESH,
        )

    def two(g, first, half, k):
        place = half_x.at[across, pl.ds(first // 2, half)]
        return pltpu.make_async_remote_copy(
            src_ref=place,
            dst_ref=place,
            send_sem=two_send.at[g, k],
            recv_sem=two_recv.at[g, k],
            device_id={"rep": lax.rem(across + k, pairs) * 2 + core},
            device_id_type=MESH,
        )

    def three(g, first, half):
        keep = pl.multiple_of(first + core * half, 8)
        return pltpu.make_async_remote_copy(
            src_ref=out_ref.at[pl.ds(keep, half)],
            dst_ref=out_ref.at[pl.ds(keep, half)],
            send_sem=three_send.at[g],
            recv_sem=three_recv.at[g],
            device_id={"rep": sibling},
            device_id_type=MESH,
        )

    def stage_two(g, first, half):
        one(g, first, half).wait()
        keep = pl.ds(pl.multiple_of(first + core * half, 8), half)
        half_x[across, pl.ds(first // 2, half)] = acc[keep] + half_in[pl.ds(first // 2, half)]
        for k in range(1, pairs):
            two(g, first, half, k).start()

    def stage_three(g, first, half):
        for k in range(1, pairs):
            two(g, first, half, k).wait()
        total = half_x[0, pl.ds(first // 2, half)]
        for k in range(1, pairs):
            total = total + half_x[k, pl.ds(first // 2, half)]
        out_ref[pl.ds(pl.multiple_of(first + core * half, 8), half)] = total
        three(g, first, half).start()

    groups = [(0, 0, (width + HEADS) // 2)]
    for k in range(1, depth):
        groups.append((k, groups[-1][1] + 2 * groups[-1][2], width // 2))
    groups.append((depth, groups[-1][1] + 2 * groups[-1][2], feats // 2))

    def top_layer(q, carry):
        part = cols(q * chunk)
        for k in range(1, volumes):
            seg_copy(q, k).wait()
        own_rank = rank_ref[pl.ds(mine, 1), part]
        ranks = rank_ref[:, part]
        logs = [seg[u, 1:2, part] for u in range(volumes)]
        summed = jnp.zeros(ranks.shape, F32)
        for u in range(volumes):
            summed = summed + jnp.where(ranks[u : u + 1] < ranks, logs[u], 0.0)
        prefix = jnp.exp(summed)
        behind = jnp.zeros((1, chunk), F32)
        own_log = jnp.zeros((1, chunk), F32)
        for u in range(volumes):
            term = prefix[u : u + 1] * seg[u, 0:1, part]
            behind = behind + jnp.where(ranks[u : u + 1] > own_rank, term, 0.0)
            own_log = own_log + jnp.where(ranks[u : u + 1] < own_rank, logs[u], 0.0)
        own = jnp.exp(own_log)
        cot = cot_ref[:, part] * own
        first_row = lax.broadcasted_iota(jnp.int32, (8, chunk), 0) == 0
        later = jnp.zeros((1, chunk), F32)
        outer = jnp.zeros((width, width), F32)
        outer_last = jnp.zeros((HEADS, width), F32)
        for s in reversed(range(samples)):
            place = cols(s * rays + q * chunk)
            gate = gates[s, :, part]
            weight = weights[s : s + 1, part]
            face = own * facing[s : s + 1, part]
            dopt = (face * leaving[s : s + 1, part] - later - behind) * spans[s : s + 1, part]
            later = later + face * weight
            g_head = jnp.where(first_row, dopt * gate, weight * cot * gate * (1.0 - gate))
            g_head = jnp.concatenate([g_head, jnp.zeros((HEADS - 8, chunk), F32)], axis=0).astype(BF16)
            outer_last = outer_last + mul_nt(g_head, hidden[depth, :, place])
            g = (mul(last_ref[...], g_head) * slope[depth, :, place].astype(F32)).astype(BF16)
            slope[depth, :, place] = g
            outer = outer + mul_nt(hidden[depth - 1, :, place], g)
        acc[0:width] += outer
        acc[width : width + HEADS] += outer_last
        return carry

    lax.fori_loop(0, chunks, top_layer, 0)
    one(*groups[0]).start()

    def layer(k, i):
        place = pl.ds(pl.multiple_of(i * block, 128), block)
        g = (mul(mid_ref[k], slope[k + 1, :, place]) * slope[k, :, place].astype(F32)).astype(BF16)
        if k:
            slope[k, :, place] = g
        _, first, half = groups[depth - k]
        below = hidden[k - 1, :, place] if k else x_ref[:, place]
        acc[first : first + 2 * half] += mul_nt(below, g)

    for k in reversed(range(depth)):
        at = depth - 1 - k

        @pl.loop(0, 4)
        def _(i):
            layer(k, i)

        stage_two(*groups[at])
        if at:
            stage_three(*groups[at - 1])

        @pl.loop(4, 8)
        def _(i):
            layer(k, i)

        one(*groups[at + 1]).start()
    stage_three(*groups[depth - 1])
    stage_two(*groups[depth])
    stage_three(*groups[depth])
    for group in groups:
        three(*group).wait()


def per_device(
    features, deltas, counts, order_rank, cotangent, first_weight, middle_weight, last_weight
):
    volumes = lax.axis_size("vol")
    replicas = lax.axis_size("rep")
    feats, samples, rays = features.shape[1:]
    depth, width = middle_weight.shape[1:3]
    columns = samples * rays
    x = features[0].reshape(feats, columns)
    channels = last_weight.shape[2]
    last = jnp.pad(last_weight[0], ((0, 0), (0, HEADS - channels)))
    cot = jnp.pad(cotangent, ((1, 8 - channels), (0, 0)))
    dims = (volumes, replicas, samples, rays, depth, width, feats)
    rows = depth * width + HEADS + feats
    pairs = replicas // 2
    dma = pltpu.SemaphoreType.DMA
    out = pl.pallas_call(
        functools.partial(kernel, dims),
        out_shape=jax.ShapeDtypeStruct((rows, width), F32),
        in_specs=[pl.BlockSpec(memory_space=pltpu.VMEM)] * 10,
        out_specs=pl.BlockSpec(memory_space=pltpu.VMEM),
        scratch_shapes=[
            pltpu.VMEM((depth + 1, width, columns), BF16),
            pltpu.VMEM((depth + 1, width, columns), BF16),
            pltpu.VMEM((samples, 8, rays), F32),
            pltpu.VMEM((samples, rays), F32),
            pltpu.VMEM((samples, rays), F32),
            pltpu.VMEM((samples, rays), F32),
            pltpu.VMEM((samples, rays), F32),
            pltpu.VMEM((volumes, 2, rays), F32),
            pltpu.VMEM((rows, width), F32),
            pltpu.VMEM((rows // 2, width), F32),
            pltpu.VMEM((pairs, rows // 2, width), F32),
            dma((4, volumes)),
            dma((4, volumes)),
            dma((depth + 1,)),
            dma((depth + 1,)),
            dma((depth + 1, pairs)),
            dma((depth + 1, pairs)),
            dma((depth + 1,)),
            dma((depth + 1,)),
        ],
        compiler_params=pltpu.CompilerParams(
            collective_id=0, has_side_effects=True, vmem_limit_bytes=48 * 1024 * 1024
        ),
    )(
        x,
        deltas[0],
        counts,
        order_rank.T,
        cot,
        first_weight[0].T,
        jnp.swapaxes(middle_weight[0], 1, 2),
        last.T,
        middle_weight[0],
        last,
    )
    top = width + HEADS
    middle = [out[top + (k - 1) * width : top + k * width] for k in range(depth - 1, 0, -1)]
    middle.append(out[:width])
    first_grad = out[rows - feats :]
    last_grad = out[width : width + channels].T
    return (first_grad[None], jnp.stack(middle, axis=0)[None], last_grad[None])


def solution(mesh):
    placed = (
        P("vol", None, None, "rep"),
        P("vol", None, "rep"),
        P("vol", "rep"),
        P("rep", None),
        P(None, "rep"),
        P("vol", None, None),
        P("vol", None, None, None),
        P("vol", None, None),
    )
    return jax.shard_map(
        per_device,
        mesh=mesh,
        in_specs=placed,
        out_specs=(P("vol", None, None), P("vol", None, None, None), P("vol", None, None)),
        check_vma=False,
    )
```

```python
import functools

import jax
import jax.numpy as jnp
from jax import lax
from jax.experimental import pallas as pl
from jax.experimental.pallas import tpu as pltpu
from jax.sharding import PartitionSpec as P

F32 = jnp.float32
BF16 = jnp.bfloat16
MESH = pl.DeviceIdType.MESH
HEADS = 16


def mul(left, right):
    return jnp.dot(left, right, preferred_element_type=F32)


def mul_nt(left, right):
    return lax.dot_general(left, right, (((1,), (1,)), ((), ())), preferred_element_type=F32)


def logistic(pre):
    return 0.5 * jnp.tanh(0.5 * pre) + 0.5


def activate(half):
    twice = jnp.tanh(half) + 1.0
    hidden = half * twice
    slope = twice + hidden * (2.0 - twice)
    return hidden.astype(BF16), slope.astype(BF16)


def kernel(
    dims,
    x_ref, deltas_ref, counts_ref, rank_ref, cot_ref,
    first_t_ref, mid_t_ref, last_t_ref, mid_ref, last_ref,
    middle_ref, small_ref,
    hidden, slope, gates, leaving, weights, spans, facing, seg, acc, half_in, half_x,
    seg_send, seg_recv, one_send, one_recv, two_send, two_recv, three_send, three_recv,
):
    volumes, replicas, samples, rays, depth, width, feats = dims
    chunk = rays // 4
    chunks = rays // chunk
    columns = samples * rays
    block = columns // 8
    pairs = replicas // 2
    mine = lax.axis_index("vol")
    rep = lax.axis_index("rep")
    core = lax.rem(rep, 2)
    across = rep // 2
    sibling = rep + 1 - 2 * core

    barrier = pltpu.get_barrier_semaphore()
    for k in range(1, volumes):
        pl.semaphore_signal(
            barrier, inc=1, device_id={"vol": lax.rem(mine + k, volumes)}, device_id_type=MESH
        )
    pl.semaphore_signal(barrier, inc=1, device_id={"rep": sibling}, device_id_type=MESH)
    for k in range(1, pairs):
        pl.semaphore_signal(
            barrier,
            inc=1,
            device_id={"rep": lax.rem(across + k, pairs) * 2 + core},
            device_id_type=MESH,
        )
    def cols(start):
        return pl.ds(pl.multiple_of(start, 128), chunk)

    def seg_copy(q, k):
        part = cols(q * chunk)
        return pltpu.make_async_remote_copy(
            src_ref=seg.at[mine, :, part],
            dst_ref=seg.at[mine, :, part],
            send_sem=seg_send.at[q, k],
            recv_sem=seg_recv.at[q, k],
            device_id={"vol": lax.rem(mine + k, volumes)},
            device_id_type=MESH,
        )

    def padded(cot):
        below = jnp.zeros((7 - cot.shape[0], cot.shape[1]), F32)
        return jnp.concatenate([jnp.zeros((1, cot.shape[1]), F32), cot, below], axis=0)

    acc[...] = jnp.zeros_like(acc)

    def forward(q, carry):
        part = cols(q * chunk)
        cot = padded(cot_ref[:, part])
        count = counts_ref[:, part]
        places = [cols(s * rays + q * chunk) for s in range(samples)]
        below = [x_ref[:, place] for place in places]
        for k in range(depth + 1):
            matrix = mid_t_ref[k - 1] if k else first_t_ref[...]
            above = []
            for s, place in enumerate(places):
                h, d = activate(mul(matrix, below[s]))
                hidden[k, :, place] = h
                slope[k, :, place] = d
                above.append(h)
            below = above
        heads = [mul(last_t_ref[...], h)[:8] for h in below]
        reached = jnp.zeros((1, chunk), F32)
        before = jnp.ones((1, chunk), F32)
        colour = jnp.zeros((1, chunk), F32)
        for s in range(samples):
            gate = logistic(heads[s])
            top = heads[s][0:1]
            density = jnp.maximum(top, 0.0) + jnp.log1p(jnp.exp(-jnp.abs(top)))
            span = jnp.where(s < count, deltas_ref[s : s + 1, part], 0.0)
            reached = reached + density * span
            after = jnp.exp(-reached)
            weight = before - after
            before = after
            face = jnp.sum(cot * gate, axis=0, keepdims=True)
            colour = colour + weight * face
            gates[s, :, part] = gate
            leaving[s : s + 1, part] = after
            weights[s : s + 1, part] = weight
            spans[s : s + 1, part] = span
            facing[s : s + 1, part] = face
        seg[mine, :, part] = jnp.concatenate([colour, -reached], axis=0)

        @pl.when(q == 0)
        def _():
            pl.semaphore_wait(barrier, volumes - 1 + pairs)

        for k in range(1, volumes):
            seg_copy(q, k).start()
        return carry

    lax.fori_loop(0, chunks, forward, 0)

    def one(g, first, half):
        give = pl.multiple_of(first + (1 - core) * half, 8)
        return pltpu.make_async_remote_copy(
            src_ref=acc.at[pl.ds(give, half)],
            dst_ref=half_in.at[pl.ds(first // 2, half)],
            send_sem=one_send.at[g],
            recv_sem=one_recv.at[g],
            device_id={"rep": sibling},
            device_id_type=MESH,
        )

    def two(g, first, half, k):
        place = half_x.at[across, pl.ds(first // 2, half)]
        return pltpu.make_async_remote_copy(
            src_ref=place,
            dst_ref=place,
            send_sem=two_send.at[g, k],
            recv_sem=two_recv.at[g, k],
            device_id={"rep": lax.rem(across + k, pairs) * 2 + core},
            device_id_type=MESH,
        )

    def landing(g, half):
        rows = pl.ds(pl.multiple_of(core * half, 8), half)
        return small_ref.at[rows] if g == depth else middle_ref.at[depth - 1 - g, rows]

    def three(g, first, half):
        return pltpu.make_async_remote_copy(
            src_ref=landing(g, half),
            dst_ref=landing(g, half),
            send_sem=three_send.at[g],
            recv_sem=three_recv.at[g],
            device_id={"rep": sibling},
            device_id_type=MESH,
        )

    def stage_two(g, first, half):
        one(g, first, half).wait()
        keep = pl.ds(pl.multiple_of(first + core * half, 8), half)
        half_x[across, pl.ds(first // 2, half)] = acc[keep] + half_in[pl.ds(first // 2, half)]
        for k in range(1, pairs):
            two(g, first, half, k).start()

    def stage_three(g, first, half):
        for k in range(1, pairs):
            two(g, first, half, k).wait()
        total = half_x[0, pl.ds(first // 2, half)]
        for k in range(1, pairs):
            total = total + half_x[k, pl.ds(first // 2, half)]
        landing(g, half)[...] = total
        three(g, first, half).start()

    groups = [(k, k * width, width // 2) for k in range(depth)]
    groups.append((depth, depth * width, (feats + HEADS) // 2))

    def top_layer(q, carry):
        part = cols(q * chunk)
        for k in range(1, volumes):
            seg_copy(q, k).wait()
        own_rank = rank_ref[pl.ds(mine, 1), part]
        ranks = rank_ref[:, part]
        logs = [seg[u, 1:2, part] for u in range(volumes)]
        summed = jnp.zeros(ranks.shape, F32)
        for u in range(volumes):
            summed = summed + jnp.where(ranks[u : u + 1] < ranks, logs[u], 0.0)
        prefix = jnp.exp(summed)
        behind = jnp.zeros((1, chunk), F32)
        own_log = jnp.zeros((1, chunk), F32)
        for u in range(volumes):
            term = prefix[u : u + 1] * seg[u, 0:1, part]
            behind = behind + jnp.where(ranks[u : u + 1] > own_rank, term, 0.0)
            own_log = own_log + jnp.where(ranks[u : u + 1] < own_rank, logs[u], 0.0)
        own = jnp.exp(own_log)
        cot = padded(cot_ref[:, part]) * own
        first_row = lax.broadcasted_iota(jnp.int32, (8, chunk), 0) == 0
        later = jnp.zeros((1, chunk), F32)
        outer = jnp.zeros((width, width), F32)
        outer_last = jnp.zeros((HEADS, width), F32)
        for s in reversed(range(samples)):
            place = cols(s * rays + q * chunk)
            gate = gates[s, :, part]
            weight = weights[s : s + 1, part]
            face = own * facing[s : s + 1, part]
            dopt = (face * leaving[s : s + 1, part] - later - behind) * spans[s : s + 1, part]
            later = later + face * weight
            g_head = jnp.where(first_row, dopt * gate, weight * cot * gate * (1.0 - gate))
            g_head = jnp.concatenate([g_head, jnp.zeros((HEADS - 8, chunk), F32)], axis=0).astype(BF16)
            outer_last = outer_last + mul_nt(g_head, hidden[depth, :, place])
            g = (mul(last_ref[...], g_head) * slope[depth, :, place].astype(F32)).astype(BF16)
            slope[depth, :, place] = g
            outer = outer + mul_nt(hidden[depth - 1, :, place], g)
        acc[0:width] += outer
        acc[depth * width + feats :] += outer_last
        return carry

    lax.fori_loop(0, chunks, top_layer, 0)
    one(*groups[0]).start()

    def layer(k, i):
        place = pl.ds(pl.multiple_of(i * block, 128), block)
        g = (mul(mid_ref[k], slope[k + 1, :, place]) * slope[k, :, place].astype(F32)).astype(BF16)
        if k:
            slope[k, :, place] = g
        first = (depth - k) * width
        below = hidden[k - 1, :, place] if k else x_ref[:, place]
        acc[first : first + below.shape[0]] += mul_nt(below, g)

    for k in reversed(range(depth)):
        at = depth - 1 - k

        @pl.loop(0, 4)
        def _(i):
            layer(k, i)

        stage_two(*groups[at])
        if at:
            stage_three(*groups[at - 1])

        @pl.loop(4, 8)
        def _(i):
            layer(k, i)

        one(*groups[at + 1]).start()
    stage_three(*groups[depth - 1])
    stage_two(*groups[depth])
    stage_three(*groups[depth])
    for group in groups:
        three(*group).wait()


def per_device(
    features, deltas, counts, order_rank, cotangent, first_weight, middle_weight, last_weight
):
    volumes = lax.axis_size("vol")
    replicas = lax.axis_size("rep")
    feats, samples, rays = features.shape[1:]
    depth, width = middle_weight.shape[1:3]
    columns = samples * rays
    x = features[0].reshape(feats, columns)
    channels = last_weight.shape[2]
    last = jnp.pad(last_weight[0], ((0, 0), (0, HEADS - channels)))
    half = jnp.asarray(0.5, BF16)
    middle = middle_weight[0] * half
    dims = (volumes, replicas, samples, rays, depth, width, feats)
    rows = depth * width + HEADS + feats
    pairs = replicas // 2
    dma = pltpu.SemaphoreType.DMA
    middle_grad, small = pl.pallas_call(
        functools.partial(kernel, dims),
        out_shape=(
            jax.ShapeDtypeStruct((depth, width, width), F32),
            jax.ShapeDtypeStruct((feats + HEADS, width), F32),
        ),
        in_specs=[pl.BlockSpec(memory_space=pltpu.VMEM)] * 10,
        out_specs=(pl.BlockSpec(memory_space=pltpu.VMEM),) * 2,
        scratch_shapes=[
            pltpu.VMEM((depth + 1, width, columns), BF16),
            pltpu.VMEM((depth + 1, width, columns), BF16),
            pltpu.VMEM((samples, 8, rays), F32),
            pltpu.VMEM((samples, rays), F32),
            pltpu.VMEM((samples, rays), F32),
            pltpu.VMEM((samples, rays), F32),
            pltpu.VMEM((samples, rays), F32),
            pltpu.VMEM((volumes, 2, rays), F32),
            pltpu.VMEM((rows, width), F32),
            pltpu.VMEM((rows // 2, width), F32),
            pltpu.VMEM((pairs, rows // 2, width), F32),
            dma((4, volumes)),
            dma((4, volumes)),
            dma((depth + 1,)),
            dma((depth + 1,)),
            dma((depth + 1, pairs)),
            dma((depth + 1, pairs)),
            dma((depth + 1,)),
            dma((depth + 1,)),
        ],
        compiler_params=pltpu.CompilerParams(
            collective_id=0, has_side_effects=True, vmem_limit_bytes=48 * 1024 * 1024
        ),
    )(
        x,
        deltas[0],
        counts,
        order_rank.T,
        cotangent,
        first_weight[0].T * half,
        jnp.swapaxes(middle, 1, 2),
        last.T,
        middle,
        last * half,
    )
    first_grad = small[:feats]
    last_grad = small[feats : feats + channels].T
    return (first_grad[None], middle_grad[None], last_grad[None])


def solution(mesh):
    placed = (
        P("vol", None, None, "rep"),
        P("vol", None, "rep"),
        P("vol", "rep"),
        P("rep", None),
        P(None, "rep"),
        P("vol", None, None),
        P("vol", None, None, None),
        P("vol", None, None),
    )
    return jax.shard_map(
        per_device,
        mesh=mesh,
        in_specs=placed,
        out_specs=(P("vol", None, None), P("vol", None, None, None), P("vol", None, None)),
        check_vma=False,
    )
```

```python
import functools

import jax
import jax.numpy as jnp
from jax import lax
from jax.experimental import pallas as pl
from jax.experimental.pallas import tpu as pltpu
from jax.sharding import PartitionSpec as P

F32 = jnp.float32
BF16 = jnp.bfloat16
MESH = pl.DeviceIdType.MESH
HEADS = 16


def mul(left, right):
    return jnp.dot(left, right, preferred_element_type=F32)


def mul_nt(left, right):
    return lax.dot_general(left, right, (((1,), (1,)), ((), ())), preferred_element_type=F32)


def logistic(pre):
    return 0.5 * jnp.tanh(0.5 * pre) + 0.5


def activate(half):
    twice = jnp.tanh(half) + 1.0
    hidden = half * twice
    slope = twice + hidden * (2.0 - twice)
    return hidden.astype(BF16), slope.astype(BF16)


def kernel(
    dims,
    x_ref, deltas_ref, counts_ref, rank_ref, cot_ref,
    first_t_ref, mid_t_ref, last_t_ref, mid_ref, last_ref,
    middle_ref, small_ref,
    hidden, slope, gates, leaving, weights, spans, facing, seg, acc, half_in, half_x, small_in,
    seg_send, seg_recv, one_send, one_recv, two_send, two_recv, three_send, three_recv, all_send, all_recv,
):
    volumes, replicas, samples, rays, depth, width, feats = dims
    chunk = rays // 4
    chunks = rays // chunk
    columns = samples * rays
    block = columns // 8
    pairs = replicas // 2
    mine = lax.axis_index("vol")
    rep = lax.axis_index("rep")
    core = lax.rem(rep, 2)
    across = rep // 2
    sibling = rep + 1 - 2 * core

    barrier = pltpu.get_barrier_semaphore()
    for k in range(1, volumes):
        pl.semaphore_signal(
            barrier, inc=1, device_id={"vol": lax.rem(mine + k, volumes)}, device_id_type=MESH
        )
    for k in range(1, replicas):
        pl.semaphore_signal(
            barrier, inc=1, device_id={"rep": lax.rem(rep + k, replicas)}, device_id_type=MESH
        )

    def cols(start):
        return pl.ds(pl.multiple_of(start, 128), chunk)

    def seg_copy(q, k):
        part = cols(q * chunk)
        return pltpu.make_async_remote_copy(
            src_ref=seg.at[mine, :, part],
            dst_ref=seg.at[mine, :, part],
            send_sem=seg_send.at[q, k],
            recv_sem=seg_recv.at[q, k],
            device_id={"vol": lax.rem(mine + k, volumes)},
            device_id_type=MESH,
        )

    def padded(cot):
        below = jnp.zeros((7 - cot.shape[0], cot.shape[1]), F32)
        return jnp.concatenate([jnp.zeros((1, cot.shape[1]), F32), cot, below], axis=0)

    acc[...] = jnp.zeros_like(acc)

    def forward(q, carry):
        part = cols(q * chunk)
        cot = padded(cot_ref[:, part])
        count = counts_ref[:, part]
        places = [cols(s * rays + q * chunk) for s in range(samples)]
        below = [x_ref[:, place] for place in places]
        for k in range(depth + 1):
            matrix = mid_t_ref[k - 1] if k else first_t_ref[...]
            above = []
            for s, place in enumerate(places):
                h, d = activate(mul(matrix, below[s]))
                hidden[k, :, place] = h
                slope[k, :, place] = d
                above.append(h)
            below = above
        heads = [mul(last_t_ref[...], h)[:8] for h in below]
        reached = jnp.zeros((1, chunk), F32)
        before = jnp.ones((1, chunk), F32)
        colour = jnp.zeros((1, chunk), F32)
        for s in range(samples):
            gate = logistic(heads[s])
            top = heads[s][0:1]
            density = jnp.maximum(top, 0.0) + jnp.log1p(jnp.exp(-jnp.abs(top)))
            span = jnp.where(s < count, deltas_ref[s : s + 1, part], 0.0)
            reached = reached + density * span
            after = jnp.exp(-reached)
            weight = before - after
            before = after
            face = jnp.sum(cot * gate, axis=0, keepdims=True)
            colour = colour + weight * face
            gates[s, :, part] = gate
            leaving[s : s + 1, part] = after
            weights[s : s + 1, part] = weight
            spans[s : s + 1, part] = span
            facing[s : s + 1, part] = face
        seg[mine, :, part] = jnp.concatenate([colour, -reached], axis=0)

        @pl.when(q == 0)
        def _():
            pl.semaphore_wait(barrier, volumes - 1 + replicas - 1)

        for k in range(1, volumes):
            seg_copy(q, k).start()
        return carry

    lax.fori_loop(0, chunks, forward, 0)

    def one(g, first, half):
        give = pl.multiple_of(first + (1 - core) * half, 8)
        return pltpu.make_async_remote_copy(
            src_ref=acc.at[pl.ds(give, half)],
            dst_ref=half_in.at[pl.ds(first // 2, half)],
            send_sem=one_send.at[g],
            recv_sem=one_recv.at[g],
            device_id={"rep": sibling},
            device_id_type=MESH,
        )

    def two(g, first, half, k):
        place = half_x.at[across, pl.ds(first // 2, half)]
        return pltpu.make_async_remote_copy(
            src_ref=place,
            dst_ref=place,
            send_sem=two_send.at[g, k],
            recv_sem=two_recv.at[g, k],
            device_id={"rep": lax.rem(across + k, pairs) * 2 + core},
            device_id_type=MESH,
        )

    def landing(g, half):
        rows = pl.ds(pl.multiple_of(core * half, 8), half)
        return middle_ref.at[depth - 1 - g, rows]

    def three(g, first, half):
        return pltpu.make_async_remote_copy(
            src_ref=landing(g, half),
            dst_ref=landing(g, half),
            send_sem=three_send.at[g],
            recv_sem=three_recv.at[g],
            device_id={"rep": sibling},
            device_id_type=MESH,
        )

    def stage_two(g, first, half):
        one(g, first, half).wait()
        keep = pl.ds(pl.multiple_of(first + core * half, 8), half)
        half_x[across, pl.ds(first // 2, half)] = acc[keep] + half_in[pl.ds(first // 2, half)]
        for k in range(1, pairs):
            two(g, first, half, k).start()

    def stage_three(g, first, half):
        for k in range(1, pairs):
            two(g, first, half, k).wait()
        total = half_x[0, pl.ds(first // 2, half)]
        for k in range(1, pairs):
            total = total + half_x[k, pl.ds(first // 2, half)]
        landing(g, half)[...] = total
        three(g, first, half).start()

    groups = [(k, k * width, width // 2) for k in range(depth)]
    pieces = [(feats, HEADS), (0, feats)]

    def whole(p, k):
        first, count = pieces[p]
        return pltpu.make_async_remote_copy(
            src_ref=acc.at[pl.ds(depth * width + first, count)],
            dst_ref=small_in.at[rep, pl.ds(first, count)],
            send_sem=all_send.at[p, k],
            recv_sem=all_recv.at[p, k],
            device_id={"rep": lax.rem(rep + k, replicas)},
            device_id_type=MESH,
        )

    def push(p):
        for k in range(1, replicas):
            whole(p, k).start()
        first, count = pieces[p]
        rows = pl.ds(first, count)
        small_in[rep, rows] = acc[pl.ds(depth * width + first, count)]

    def collect(p):
        for k in range(1, replicas):
            whole(p, k).wait()
        first, count = pieces[p]
        rows = pl.ds(first, count)
        total = small_in[0, rows]
        for j in range(1, replicas):
            total = total + small_in[j, rows]
        small_ref[rows] = total

    def top_layer(q, carry):
        part = cols(q * chunk)
        for k in range(1, volumes):
            seg_copy(q, k).wait()
        own_rank = rank_ref[pl.ds(mine, 1), part]
        ranks = rank_ref[:, part]
        logs = [seg[u, 1:2, part] for u in range(volumes)]
        summed = jnp.zeros(ranks.shape, F32)
        for u in range(volumes):
            summed = summed + jnp.where(ranks[u : u + 1] < ranks, logs[u], 0.0)
        prefix = jnp.exp(summed)
        behind = jnp.zeros((1, chunk), F32)
        own_log = jnp.zeros((1, chunk), F32)
        for u in range(volumes):
            term = prefix[u : u + 1] * seg[u, 0:1, part]
            behind = behind + jnp.where(ranks[u : u + 1] > own_rank, term, 0.0)
            own_log = own_log + jnp.where(ranks[u : u + 1] < own_rank, logs[u], 0.0)
        own = jnp.exp(own_log)
        cot = padded(cot_ref[:, part]) * own
        first_row = lax.broadcasted_iota(jnp.int32, (8, chunk), 0) == 0
        later = jnp.zeros((1, chunk), F32)
        outer = jnp.zeros((width, width), F32)
        outer_last = jnp.zeros((HEADS, width), F32)
        for s in reversed(range(samples)):
            place = cols(s * rays + q * chunk)
            gate = gates[s, :, part]
            weight = weights[s : s + 1, part]
            face = own * facing[s : s + 1, part]
            dopt = (face * leaving[s : s + 1, part] - later - behind) * spans[s : s + 1, part]
            later = later + face * weight
            g_head = jnp.where(first_row, dopt * gate, weight * cot * gate * (1.0 - gate))
            g_head = jnp.concatenate([g_head, jnp.zeros((HEADS - 8, chunk), F32)], axis=0).astype(BF16)
            outer_last = outer_last + mul_nt(g_head, hidden[depth, :, place])
            g = (mul(last_ref[...], g_head) * slope[depth, :, place].astype(F32)).astype(BF16)
            slope[depth, :, place] = g
            outer = outer + mul_nt(hidden[depth - 1, :, place], g)
        acc[0:width] += outer
        acc[depth * width + feats :] += outer_last
        return carry

    lax.fori_loop(0, chunks, top_layer, 0)
    one(*groups[0]).start()
    push(0)

    def layer(k, i):
        place = pl.ds(pl.multiple_of(i * block, 128), block)
        g = (mul(mid_ref[k], slope[k + 1, :, place]) * slope[k, :, place].astype(F32)).astype(BF16)
        if k:
            slope[k, :, place] = g
        first = (depth - k) * width
        below = hidden[k - 1, :, place] if k else x_ref[:, place]
        acc[first : first + below.shape[0]] += mul_nt(below, g)

    for k in reversed(range(depth)):
        at = depth - 1 - k

        @pl.loop(0, 2)
        def _(i):
            layer(k, i)

        stage_two(*groups[at])
        if at:
            stage_three(*groups[at - 1])

        @pl.loop(2, 8)
        def _(i):
            layer(k, i)

        if k:
            one(*groups[at + 1]).start()
    push(1)
    stage_three(*groups[depth - 1])
    collect(0)
    collect(1)
    for group in groups:
        three(*group).wait()


def per_device(
    features, deltas, counts, order_rank, cotangent, first_weight, middle_weight, last_weight
):
    volumes = lax.axis_size("vol")
    replicas = lax.axis_size("rep")
    feats, samples, rays = features.shape[1:]
    depth, width = middle_weight.shape[1:3]
    columns = samples * rays
    x = features[0].reshape(feats, columns)
    channels = last_weight.shape[2]
    last = jnp.pad(last_weight[0], ((0, 0), (0, HEADS - channels)))
    half = jnp.asarray(0.5, BF16)
    middle = middle_weight[0] * half
    dims = (volumes, replicas, samples, rays, depth, width, feats)
    rows = depth * width + HEADS + feats
    pairs = replicas // 2
    dma = pltpu.SemaphoreType.DMA
    middle_grad, small = pl.pallas_call(
        functools.partial(kernel, dims),
        out_shape=(
            jax.ShapeDtypeStruct((depth, width, width), F32),
            jax.ShapeDtypeStruct((feats + HEADS, width), F32),
        ),
        in_specs=[pl.BlockSpec(memory_space=pltpu.VMEM)] * 10,
        out_specs=(pl.BlockSpec(memory_space=pltpu.VMEM),) * 2,
        scratch_shapes=[
            pltpu.VMEM((depth + 1, width, columns), BF16),
            pltpu.VMEM((depth + 1, width, columns), BF16),
            pltpu.VMEM((samples, 8, rays), F32),
            pltpu.VMEM((samples, rays), F32),
            pltpu.VMEM((samples, rays), F32),
            pltpu.VMEM((samples, rays), F32),
            pltpu.VMEM((samples, rays), F32),
            pltpu.VMEM((volumes, 2, rays), F32),
            pltpu.VMEM((rows, width), F32),
            pltpu.VMEM((depth * width // 2, width), F32),
            pltpu.VMEM((pairs, depth * width // 2, width), F32),
            pltpu.VMEM((replicas, feats + HEADS, width), F32),
            dma((4, volumes)),
            dma((4, volumes)),
            dma((depth,)),
            dma((depth,)),
            dma((depth, pairs)),
            dma((depth, pairs)),
            dma((depth,)),
            dma((depth,)),
            dma((2, replicas)),
            dma((2, replicas)),
        ],
        compiler_params=pltpu.CompilerParams(
            collective_id=0, has_side_effects=True, vmem_limit_bytes=48 * 1024 * 1024
        ),
    )(
        x,
        deltas[0],
        counts,
        order_rank.T,
        cotangent,
        first_weight[0].T * half,
        jnp.swapaxes(middle, 1, 2),
        last.T,
        middle,
        last * half,
    )
    first_grad = small[:feats]
    last_grad = small[feats : feats + channels].T
    return (first_grad[None], middle_grad[None], last_grad[None])


def solution(mesh):
    placed = (
        P("vol", None, None, "rep"),
        P("vol", None, "rep"),
        P("vol", "rep"),
        P("rep", None),
        P(None, "rep"),
        P("vol", None, None),
        P("vol", None, None, None),
        P("vol", None, None),
    )
    return jax.shard_map(
        per_device,
        mesh=mesh,
        in_specs=placed,
        out_specs=(P("vol", None, None), P("vol", None, None, None), P("vol", None, None)),
        check_vma=False,
    )
```

```python
import functools

import jax
import jax.numpy as jnp
from jax import lax
from jax.experimental import pallas as pl
from jax.experimental.pallas import tpu as pltpu
from jax.sharding import PartitionSpec as P

F32 = jnp.float32
BF16 = jnp.bfloat16
MESH = pl.DeviceIdType.MESH
HEADS = 16


def mul(left, right):
    return jnp.dot(left, right, preferred_element_type=F32)


def mul_nt(left, right):
    return lax.dot_general(left, right, (((1,), (1,)), ((), ())), preferred_element_type=F32)


def logistic(pre):
    return 0.5 * jnp.tanh(0.5 * pre) + 0.5


def activate(half):
    twice = jnp.tanh(half) + 1.0
    hidden = half * twice
    slope = twice + hidden * (2.0 - twice)
    return hidden.astype(BF16), slope.astype(BF16)


def kernel(
    dims,
    x_ref, deltas_ref, counts_ref, rank_ref, cot_ref,
    first_t_ref, mid_t_ref, last_t_ref, mid_ref, last_ref,
    middle_ref, small_ref,
    hidden, slope, gates, leaving, weights, spans, facing, seg, acc, half_in, half_x, small_in,
    seg_send, seg_recv, one_send, one_recv, two_send, two_recv, three_send, three_recv, all_send, all_recv,
):
    volumes, replicas, samples, rays, depth, width, feats = dims
    chunk = rays // 4
    chunks = rays // chunk
    columns = samples * rays
    block = columns // 4
    pairs = replicas // 2
    mine = lax.axis_index("vol")
    rep = lax.axis_index("rep")
    core = lax.rem(rep, 2)
    across = rep // 2
    sibling = rep + 1 - 2 * core

    barrier = pltpu.get_barrier_semaphore()
    for k in range(1, volumes):
        pl.semaphore_signal(
            barrier, inc=1, device_id={"vol": lax.rem(mine + k, volumes)}, device_id_type=MESH
        )
    for k in range(1, replicas):
        pl.semaphore_signal(
            barrier, inc=1, device_id={"rep": lax.rem(rep + k, replicas)}, device_id_type=MESH
        )

    def cols(start):
        return pl.ds(pl.multiple_of(start, 128), chunk)

    def seg_copy(q, k):
        part = cols(q * chunk)
        return pltpu.make_async_remote_copy(
            src_ref=seg.at[mine, :, part],
            dst_ref=seg.at[mine, :, part],
            send_sem=seg_send.at[q, k],
            recv_sem=seg_recv.at[q, k],
            device_id={"vol": lax.rem(mine + k, volumes)},
            device_id_type=MESH,
        )

    def padded(cot):
        below = jnp.zeros((7 - cot.shape[0], cot.shape[1]), F32)
        return jnp.concatenate([jnp.zeros((1, cot.shape[1]), F32), cot, below], axis=0)

    acc[...] = jnp.zeros_like(acc)

    def forward(q, carry):
        part = cols(q * chunk)
        cot = padded(cot_ref[:, part])
        count = counts_ref[:, part]
        places = [cols(s * rays + q * chunk) for s in range(samples)]
        below = [x_ref[:, place] for place in places]
        for k in range(depth + 1):
            matrix = mid_t_ref[k - 1] if k else first_t_ref[...]
            above = []
            for s, place in enumerate(places):
                h, d = activate(mul(matrix, below[s]))
                hidden[k, :, place] = h
                slope[k, :, place] = d
                above.append(h)
            below = above
        heads = [mul(last_t_ref[...], h)[:8] for h in below]
        reached = jnp.zeros((1, chunk), F32)
        before = jnp.ones((1, chunk), F32)
        colour = jnp.zeros((1, chunk), F32)
        for s in range(samples):
            gate = logistic(heads[s])
            top = heads[s][0:1]
            density = jnp.maximum(top, 0.0) + jnp.log1p(jnp.exp(-jnp.abs(top)))
            span = jnp.where(s < count, deltas_ref[s : s + 1, part], 0.0)
            reached = reached + density * span
            after = jnp.exp(-reached)
            weight = before - after
            before = after
            face = jnp.sum(cot * gate, axis=0, keepdims=True)
            colour = colour + weight * face
            gates[s, :, part] = gate
            leaving[s : s + 1, part] = after
            weights[s : s + 1, part] = weight
            spans[s : s + 1, part] = span
            facing[s : s + 1, part] = face
        seg[mine, :, part] = jnp.concatenate([colour, -reached], axis=0)

        @pl.when(q == 0)
        def _():
            pl.semaphore_wait(barrier, volumes - 1 + replicas - 1)

        for k in range(1, volumes):
            seg_copy(q, k).start()
        return carry

    lax.fori_loop(0, chunks, forward, 0)

    def one(g, first, half):
        give = pl.multiple_of(first + (1 - core) * half, 8)
        return pltpu.make_async_remote_copy(
            src_ref=acc.at[pl.ds(give, half)],
            dst_ref=half_in.at[pl.ds(first // 2, half)],
            send_sem=one_send.at[g],
            recv_sem=one_recv.at[g],
            device_id={"rep": sibling},
            device_id_type=MESH,
        )

    def two(g, first, half, k):
        place = half_x.at[across, pl.ds(first // 2, half)]
        return pltpu.make_async_remote_copy(
            src_ref=place,
            dst_ref=place,
            send_sem=two_send.at[g, k],
            recv_sem=two_recv.at[g, k],
            device_id={"rep": lax.rem(across + k, pairs) * 2 + core},
            device_id_type=MESH,
        )

    def landing(g, half):
        rows = pl.ds(pl.multiple_of(core * half, 8), half)
        return middle_ref.at[depth - 1 - g, rows]

    def three(g, first, half):
        return pltpu.make_async_remote_copy(
            src_ref=landing(g, half),
            dst_ref=landing(g, half),
            send_sem=three_send.at[g],
            recv_sem=three_recv.at[g],
            device_id={"rep": sibling},
            device_id_type=MESH,
        )

    def stage_two(g, first, half):
        one(g, first, half).wait()
        keep = pl.ds(pl.multiple_of(first + core * half, 8), half)
        half_x[across, pl.ds(first // 2, half)] = acc[keep] + half_in[pl.ds(first // 2, half)]
        for k in range(1, pairs):
            two(g, first, half, k).start()

    def stage_three(g, first, half):
        for k in range(1, pairs):
            two(g, first, half, k).wait()
        total = half_x[0, pl.ds(first // 2, half)]
        for k in range(1, pairs):
            total = total + half_x[k, pl.ds(first // 2, half)]
        landing(g, half)[...] = total
        three(g, first, half).start()

    groups = [(k, k * width, width // 2) for k in range(depth)]
    pieces = [(feats, HEADS), (0, feats)]

    def whole(p, k):
        first, count = pieces[p]
        return pltpu.make_async_remote_copy(
            src_ref=acc.at[pl.ds(depth * width + first, count)],
            dst_ref=small_in.at[rep, pl.ds(first, count)],
            send_sem=all_send.at[p, k],
            recv_sem=all_recv.at[p, k],
            device_id={"rep": lax.rem(rep + k, replicas)},
            device_id_type=MESH,
        )

    def push(p):
        for k in range(1, replicas):
            whole(p, k).start()
        first, count = pieces[p]
        rows = pl.ds(first, count)
        small_in[rep, rows] = acc[pl.ds(depth * width + first, count)]

    def collect(p):
        for k in range(1, replicas):
            whole(p, k).wait()
        first, count = pieces[p]
        rows = pl.ds(first, count)
        total = small_in[0, rows]
        for j in range(1, replicas):
            total = total + small_in[j, rows]
        small_ref[rows] = total

    def top_layer(q, carry):
        part = cols(q * chunk)
        for k in range(1, volumes):
            seg_copy(q, k).wait()
        own_rank = rank_ref[pl.ds(mine, 1), part]
        ranks = rank_ref[:, part]
        logs = [seg[u, 1:2, part] for u in range(volumes)]
        summed = jnp.zeros(ranks.shape, F32)
        for u in range(volumes):
            summed = summed + jnp.where(ranks[u : u + 1] < ranks, logs[u], 0.0)
        prefix = jnp.exp(summed)
        behind = jnp.zeros((1, chunk), F32)
        own_log = jnp.zeros((1, chunk), F32)
        for u in range(volumes):
            term = prefix[u : u + 1] * seg[u, 0:1, part]
            behind = behind + jnp.where(ranks[u : u + 1] > own_rank, term, 0.0)
            own_log = own_log + jnp.where(ranks[u : u + 1] < own_rank, logs[u], 0.0)
        own = jnp.exp(own_log)
        cot = padded(cot_ref[:, part]) * own
        first_row = lax.broadcasted_iota(jnp.int32, (8, chunk), 0) == 0
        later = jnp.zeros((1, chunk), F32)
        outer = jnp.zeros((width, width), F32)
        outer_last = jnp.zeros((HEADS, width), F32)
        for s in reversed(range(samples)):
            place = cols(s * rays + q * chunk)
            gate = gates[s, :, part]
            weight = weights[s : s + 1, part]
            face = own * facing[s : s + 1, part]
            dopt = (face * leaving[s : s + 1, part] - later - behind) * spans[s : s + 1, part]
            later = later + face * weight
            g_head = jnp.where(first_row, dopt * gate, weight * cot * gate * (1.0 - gate))
            g_head = jnp.concatenate([g_head, jnp.zeros((HEADS - 8, chunk), F32)], axis=0).astype(BF16)
            outer_last = outer_last + mul_nt(g_head, hidden[depth, :, place])
            g = (mul(last_ref[...], g_head) * slope[depth, :, place].astype(F32)).astype(BF16)
            slope[depth, :, place] = g
            outer = outer + mul_nt(hidden[depth - 1, :, place], g)
        acc[0:width] += outer
        acc[depth * width + feats :] += outer_last
        return carry

    lax.fori_loop(0, chunks, top_layer, 0)
    one(*groups[0]).start()
    push(0)

    def layer(k, i):
        place = pl.ds(pl.multiple_of(i * block, 128), block)
        g = (mul(mid_ref[k], slope[k + 1, :, place]) * slope[k, :, place].astype(F32)).astype(BF16)
        if k:
            slope[k, :, place] = g
        first = (depth - k) * width
        below = hidden[k - 1, :, place] if k else x_ref[:, place]
        acc[first : first + below.shape[0]] += mul_nt(below, g)

    for k in reversed(range(depth)):
        at = depth - 1 - k

        @pl.loop(0, 1)
        def _(i):
            layer(k, i)

        stage_two(*groups[at])
        if at:
            stage_three(*groups[at - 1])

        @pl.loop(1, 4)
        def _(i):
            layer(k, i)

        if k:
            one(*groups[at + 1]).start()
    push(1)
    stage_three(*groups[depth - 1])
    collect(0)
    collect(1)
    for group in groups:
        three(*group).wait()


def per_device(
    features, deltas, counts, order_rank, cotangent, first_weight, middle_weight, last_weight
):
    volumes = lax.axis_size("vol")
    replicas = lax.axis_size("rep")
    feats, samples, rays = features.shape[1:]
    depth, width = middle_weight.shape[1:3]
    columns = samples * rays
    x = features[0].reshape(feats, columns)
    channels = last_weight.shape[2]
    last = jnp.pad(last_weight[0], ((0, 0), (0, HEADS - channels)))
    half = jnp.asarray(0.5, BF16)
    middle = middle_weight[0] * half
    dims = (volumes, replicas, samples, rays, depth, width, feats)
    rows = depth * width + HEADS + feats
    pairs = replicas // 2
    dma = pltpu.SemaphoreType.DMA
    middle_grad, small = pl.pallas_call(
        functools.partial(kernel, dims),
        out_shape=(
            jax.ShapeDtypeStruct((depth, width, width), F32),
            jax.ShapeDtypeStruct((feats + HEADS, width), F32),
        ),
        in_specs=[pl.BlockSpec(memory_space=pltpu.VMEM)] * 10,
        out_specs=(pl.BlockSpec(memory_space=pltpu.VMEM),) * 2,
        scratch_shapes=[
            pltpu.VMEM((depth + 1, width, columns), BF16),
            pltpu.VMEM((depth + 1, width, columns), BF16),
            pltpu.VMEM((samples, 8, rays), F32),
            pltpu.VMEM((samples, rays), F32),
            pltpu.VMEM((samples, rays), F32),
            pltpu.VMEM((samples, rays), F32),
            pltpu.VMEM((samples, rays), F32),
            pltpu.VMEM((volumes, 2, rays), F32),
            pltpu.VMEM((rows, width), F32),
            pltpu.VMEM((depth * width // 2, width), F32),
            pltpu.VMEM((pairs, depth * width // 2, width), F32),
            pltpu.VMEM((replicas, feats + HEADS, width), F32),
            dma((4, volumes)),
            dma((4, volumes)),
            dma((depth,)),
            dma((depth,)),
            dma((depth, pairs)),
            dma((depth, pairs)),
            dma((depth,)),
            dma((depth,)),
            dma((2, replicas)),
            dma((2, replicas)),
        ],
        compiler_params=pltpu.CompilerParams(
            collective_id=0, has_side_effects=True, vmem_limit_bytes=48 * 1024 * 1024
        ),
    )(
        x,
        deltas[0],
        counts,
        order_rank.T,
        cotangent,
        first_weight[0].T * half,
        jnp.swapaxes(middle, 1, 2),
        last.T,
        middle,
        last * half,
    )
    first_grad = small[:feats]
    last_grad = small[feats : feats + channels].T
    return (first_grad[None], middle_grad[None], last_grad[None])


def solution(mesh):
    placed = (
        P("vol", None, None, "rep"),
        P("vol", None, "rep"),
        P("vol", "rep"),
        P("rep", None),
        P(None, "rep"),
        P("vol", None, None),
        P("vol", None, None, None),
        P("vol", None, None),
    )
    return jax.shard_map(
        per_device,
        mesh=mesh,
        in_specs=placed,
        out_specs=(P("vol", None, None), P("vol", None, None, None), P("vol", None, None)),
        check_vma=False,
    )
```
